32 devices in a mesh: groups: 2 (over x), tensor: 16 (over z, y, core).
Axes of the slice: x: 2, y: 2, z: 4, core: 2. Of those that a mesh axis runs over, the one named last changes fastest.
Arguments:
- tokens: bfloat16 [64, 7424], P(('groups', 'tensor')), parts along dimension 0, may hold values from -6 to 6
- gate_weight: bfloat16 [7424, 29696], P(None, 'tensor'), may hold values from -0.0625 to 0.0625
- up_weight: bfloat16 [7424, 29696], P(None, 'tensor'), may hold values from -0.0625 to 0.0625
- down_weight: bfloat16 [29696, 7424], P('tensor'), may hold values from -0.03125 to 0.03125
- valid_counts: int32 [32], P(('groups', 'tensor')), parts along dimension 0, may hold values from 1 to 2, 24 in all
Outputs:
- mixed: bfloat16 [64, 7424], P(('groups', 'tensor')), parts along dimension 0
The draws below stay inside these ranges and needn't reach their ends.
There are 2 independent parts, one for each index of `groups`. The reference program is written for one: setup_inputs(seed, part) draws one part's arguments, and reference() takes and returns one part's arrays. A program takes and returns all parts, laid end to end along the dimension named above; an argument that names none is the same for every part. Nothing has to cross between parts.
Inputs may be any that keep to these rules, and one draw needn't show every extreme that they name: `valid_counts`: the counts sum to 24; some block is full in every draw.
All inputs are finite; a program needn't handle non-finite values.
Results may differ from the reference program's by a relative error of at most 0.005.
Values may be sent and summed in bfloat16 or wider, within the bound.
No kernel may reach another device: no remote copies, remote signals or barrier semaphores. Data moves between devices by JAX's collectives and lax.ppermute only.
A program may use at most 192 MiB of HBM per device.

```python
import math
import jax
import jax.numpy as jnp
import numpy as np

D = 7424
FF = 29696
TOK_DEV = 2
TOKENS = 32
N_TENSOR = 16


def shard_levels(key, dims, split, smallest, largest):
    loudness = 1.0
    for axis_at, blocks in split:
        heights = jax.random.uniform(jax.random.fold_in(jax.random.fold_in(key, 6), axis_at), (blocks,), jnp.float32, smallest / len(split), largest / len(split))
        loudness = loudness * jnp.repeat(jnp.exp(heights), dims[axis_at] // blocks).reshape((-1,) + (1,) * (len(dims) - 1 - axis_at))
    return loudness


def split_up(amount, total, bound, lean):
    weights = [(1 << 20) // math.isqrt(rank ** lean) + 1 for rank in range(2, amount + 1)]
    surplus, counts = total - bound - (amount - 1), [1] * (amount - 1)
    while surplus > 0:
        candidates = [i for i in range(amount - 1) if counts[i] < bound]
        mass, remaining = sum([weights[i] for i in candidates]), surplus
        for i in candidates:
            more = min(bound - counts[i], max(1, remaining * weights[i] // mass), surplus)
            counts[i] = counts[i] + more
            surplus = surplus - more
    return np.array([bound] + counts)


def ragged_sizes(key, number_of, total, reach, skew):
    if number_of == 2:
        one = jax.random.randint(key, (), max(1, total - reach), min(reach, total - 1) + 1)
        return jnp.stack([one, total - one])
    sizes = jnp.asarray(split_up(number_of, total, reach, skew), jnp.int32)
    twos = (number_of - 1) // 2
    source_of, taker = sizes[1:1 + 2 * twos:2], sizes[2:2 + 2 * twos:2]
    room = jnp.minimum(source_of - 1, reach - taker)
    passed = jax.random.randint(jax.random.fold_in(key, 1), (twos,), 0, 1 << 20) % (room + 1)
    sizes = sizes.at[1:1 + 2 * twos:2].set(source_of - passed).at[2:2 + 2 * twos:2].set(taker + passed)
    return sizes[jax.random.permutation(jax.random.fold_in(key, 2), number_of)]


def noise(key, shape, deviation, limit, shards=(), kind=jnp.bfloat16):
    array = deviation * jax.random.normal(key, shape, jnp.float32)
    if shards:
        array = array * shard_levels(key, shape, shards, -0.22, 0.18)
    return jnp.clip(array, -limit, limit).astype(kind)


def setup_inputs(seed: int = 0, part: int = 0) -> dict:
    key_list = jax.random.split(jax.random.key(seed), 6)
    own_keys = jax.random.split(jax.random.fold_in(key_list[5], part), 6)
    tokens = noise(own_keys[0], (TOKENS, D), 1.0, 6.0, ((0, 16),))
    gate_weight = noise(key_list[1], (D, FF), D ** -0.5, 0.0625, ((1, 16),))
    up_weight = noise(key_list[2], (D, FF), D ** -0.5, 0.0625, ((1, 16),))
    down_weight = noise(key_list[3], (FF, D), FF ** -0.5, 0.03125, ((0, 16),))
    valid_counts = ragged_sizes(own_keys[4], N_TENSOR, N_TENSOR * TOK_DEV * 3 // 4, TOK_DEV, 1).astype(jnp.int32)
    return {"tokens": tokens, "gate_weight": gate_weight, "up_weight": up_weight, "down_weight": down_weight, "valid_counts": valid_counts}


def reference(tokens, gate_weight, up_weight, down_weight, valid_counts):
    position = jnp.arange(TOKENS, dtype=jnp.int32) % TOK_DEV
    block_count = jnp.repeat(valid_counts, TOK_DEV)
    keep = (position < block_count)[:, None]
    masked = jnp.where(keep, tokens, jnp.zeros_like(tokens))
    gate_value = jnp.dot(masked, gate_weight, preferred_element_type=jnp.float32)
    up_value = jnp.dot(masked, up_weight, preferred_element_type=jnp.float32)
    hidden = (jax.nn.silu(gate_value) * up_value).astype(jnp.bfloat16)
    return jnp.dot(hidden, down_weight, preferred_element_type=jnp.float32).astype(jnp.bfloat16)
```

```python
import functools

import jax
import jax.numpy as jnp
from jax import lax
from jax.experimental import pallas as pl
from jax.experimental.pallas import tpu as pltpu
from jax.sharding import PartitionSpec as P

MIB = 1 << 20
VMEM = pl.BlockSpec(memory_space=pltpu.VMEM)
HBM = pl.BlockSpec(memory_space=pltpu.HBM)
ANY = pl.BlockSpec(memory_space=pl.ANY)
BLOCKS = 4
CHUNKS = 2


def cost(flops, moved):
    return pl.CostEstimate(flops=flops, bytes_accessed=moved, transcendentals=0)


def load_kernel(start, source, after, piece, token, sem):
    copy = pltpu.make_async_copy(source.at[pl.ds(start, piece.shape[0])], piece, sem)
    copy.start()
    token[...] = jnp.zeros_like(token)
    copy.wait()


def load(source, after, start, rows):
    shape = (rows, source.shape[1])
    return pl.pallas_call(
        functools.partial(load_kernel, start),
        out_shape=(pltpu.VMEM(shape, source.dtype), jax.ShapeDtypeStruct((8, 128), jnp.float32)),
        in_specs=[HBM, VMEM],
        out_specs=(VMEM, VMEM),
        scratch_shapes=[pltpu.SemaphoreType.DMA],
        compiler_params=pltpu.CompilerParams(vmem_limit_bytes=1 * MIB),
        cost_estimate=cost(0, 2 * rows * source.shape[1]),
    )(source, after)


def join_kernel(mine, theirs, token, joined):
    rows = mine.shape[0]
    joined[:rows, :] = mine[...]
    joined[rows:, :] = theirs[...]


def join(mine, theirs, token):
    rows, width = mine.shape
    return pl.pallas_call(
        join_kernel,
        out_shape=pltpu.VMEM((2 * rows, width), mine.dtype),
        in_specs=[VMEM, VMEM, ANY],
        out_specs=VMEM,
        compiler_params=pltpu.CompilerParams(vmem_limit_bytes=2 * MIB),
        cost_estimate=cost(0, 8 * rows * width),
    )(mine, theirs, token)


def hidden_kernel(rows, mine, theirs, g0, u0, g1, u1, gate, up, down, hidden, d0, d1, d2, d3, tokens, g2, u2, g3, u3, sems):
    def copy(source, block, into, sem):
        return pltpu.make_async_copy(source.at[pl.ds(block * rows, rows)], into, sems.at[sem])

    streamed = [copy(gate, 2, g2, 0), copy(up, 2, u2, 1), copy(gate, 3, g3, 2), copy(up, 3, u3, 3)]
    for one in streamed:
        one.start()
    half = mine.shape[0]
    tokens[:half, :] = mine[...]
    tokens[half:, :] = theirs[...]
    contract = (((1,), (1,)), ((), ()))

    def compute(block, gate_block, up_block):
        half_rows = rows // 2
        gate_value = lax.dot_general(
            gate_block[...], tokens[...], contract, preferred_element_type=jnp.float32
        )
        up_value = lax.dot_general(
            up_block[...], tokens[...], contract, preferred_element_type=jnp.float32
        )
        value = gate_value / (1.0 + jnp.exp(-gate_value)) * up_value
        hidden[block * rows : (block + 1) * rows, :] = value.astype(hidden.dtype)

    later = []

    def bring(block, into):
        later.append(copy(down, block, into, 4 + block))
        later[-1].start()

    compute(0, g0, u0)
    bring(0, d0)
    bring(1, d1)
    compute(1, g1, u1)
    bring(2, d2)
    bring(3, d3)
    streamed[0].wait()
    streamed[1].wait()
    compute(2, g2, u2)
    streamed[2].wait()
    streamed[3].wait()
    compute(3, g3, u3)
    for one in later:
        one.wait()


def hidden_of(mine, theirs, pieces, gate, up, down):
    rows, width = pieces[0].shape
    count = mine.shape[0] + theirs.shape[0]
    block = pltpu.VMEM((rows, width), gate.dtype)
    return pl.pallas_call(
        functools.partial(hidden_kernel, rows),
        out_shape=(pltpu.VMEM((gate.shape[0], count), gate.dtype),) + (pltpu.VMEM((rows, width), gate.dtype),) * 4,
        in_specs=[VMEM] * 6 + [HBM] * 3,
        out_specs=(VMEM,) * 5,
        input_output_aliases={2: 1, 3: 2, 4: 3, 5: 4},
        scratch_shapes=[pltpu.VMEM((count, width), mine.dtype)] + [block] * 4 + [pltpu.SemaphoreType.DMA((8,))],
        compiler_params=pltpu.CompilerParams(vmem_limit_bytes=8 * rows * width + 4 * MIB),
        cost_estimate=cost(4 * count * gate.size, 4 * gate.size),
    )(mine, theirs, *pieces, gate, up, down)


def down_kernel(start, hidden, d0, d1, d2, d3, keep, send):
    rows, columns = d0.shape[0], keep.shape[1]
    half = keep.shape[0]
    step = 1024 if columns > 1024 else columns
    for at in range(0, columns, step):
        size = min(step, columns - at)
        total = None
        for block, piece in enumerate((d0, d1, d2, d3)):
            value = lax.dot_general(
                hidden[block * rows : (block + 1) * rows, :],
                piece[:, start + at : start + at + size],
                (((0,), (0,)), ((), ())),
                preferred_element_type=jnp.float32,
            )
            total = value if total is None else total + value
        keep[:, at : at + size] = total[:half]
        send[:, at : at + size] = total[half:].astype(send.dtype)


def down_of(hidden, pieces, start, columns):
    half = hidden.shape[1] // 2
    return pl.pallas_call(
        functools.partial(down_kernel, start),
        out_shape=(pltpu.VMEM((half, columns), jnp.float32), pltpu.VMEM((half, columns), jnp.bfloat16)),
        in_specs=[VMEM] * 5,
        out_specs=(VMEM, VMEM),
        compiler_params=pltpu.CompilerParams(vmem_limit_bytes=2 * MIB),
        cost_estimate=cost(4 * half * hidden.shape[0] * columns, 2 * hidden.shape[0] * columns),
    )(hidden, *pieces)


def exchange(array, mask, count):
    return lax.ppermute(array, "tensor", [(i, i ^ mask) for i in range(count)])


def masked(terms, own, valid_counts):
    keep = jnp.arange(own, dtype=jnp.int32)[:, None] < valid_counts[0]
    return jnp.where(keep, terms, 0.0).astype(jnp.bfloat16)


def reduced(keep, send, masks, count):
    for at, mask in enumerate(masks):
        total = keep + exchange(send, mask, count).astype(jnp.float32)
        if at + 1 == len(masks):
            return total
        rows = total.shape[0] // 2
        keep, send = total[:rows], total[rows:].astype(jnp.bfloat16)


def plain(count, masks, tokens, gate_weight, up_weight, down_weight, valid_counts):
    own = tokens.shape[0]
    gathered = tokens
    for mask in reversed(masks):
        gathered = jnp.concatenate([gathered, exchange(gathered, mask, count)], axis=0)
    gate_value = jnp.dot(gathered, gate_weight, preferred_element_type=jnp.float32)
    up_value = jnp.dot(gathered, up_weight, preferred_element_type=jnp.float32)
    hidden = (jax.nn.silu(gate_value) * up_value).astype(jnp.bfloat16)
    terms = jnp.dot(hidden, down_weight, preferred_element_type=jnp.float32)
    half = terms.shape[0] // 2
    total = reduced(terms[:half], terms[half:].astype(jnp.bfloat16), masks, count)
    return masked(total, own, valid_counts)


def per_device(count, masks, tokens, gate_weight, up_weight, down_weight, valid_counts):
    own, width = tokens.shape
    gate, up, down_weight = (
        pltpu.with_memory_space_constraint(one, pltpu.HBM)
        for one in (gate_weight.T, up_weight.T, down_weight)
    )
    rows = gate.shape[0] // BLOCKS
    mine, after, pieces = tokens, tokens, []
    wanted = [(gate, 0), (up, 0), (gate, rows), (up, rows)]
    steps = list(reversed(masks))
    for at, mask in enumerate(steps):
        theirs = exchange(mine, mask, count)
        now = wanted[:1] if at + 1 < len(steps) else wanted
        wanted = wanted[len(now) :]
        token = None
        for source, start in now:
            piece, token = load(source, after, start, rows)
            pieces.append(piece)
        if at + 1 < len(steps):
            after = mine = join(mine, theirs, token)
    hidden, *down_pieces = hidden_of(mine, theirs, pieces, gate, up, down_weight)
    columns = width // CHUNKS
    parts = []
    for chunk in range(CHUNKS):
        keep, send = down_of(hidden, down_pieces, chunk * columns, columns)
        parts.append(reduced(keep, send, masks, count))
    return masked(jnp.concatenate(parts, axis=1), own, valid_counts)


def solution(mesh):
    count = mesh.shape["tensor"]
    masks = [1 << bit for bit in range(count.bit_length() - 1)]

    def step(tokens, gate_weight, up_weight, down_weight, valid_counts):
        hidden_rows, width = down_weight.shape
        fits = 8 * hidden_rows * width <= 2 * 56 * MIB
        whole_tiles = hidden_rows % (16 * BLOCKS) == 0 and width % (128 * CHUNKS) == 0
        small = (tokens.shape[0] << len(masks)) <= 64 and len(masks) >= 4
        use = per_device if fits and whole_tiles and small else plain
        return use(count, masks, tokens, gate_weight, up_weight, down_weight, valid_counts)

    return jax.shard_map(
        step,
        mesh=mesh,
        in_specs=(
            P(("groups", "tensor"), None),
            P(None, "tensor"),
            P(None, "tensor"),
            P("tensor", None),
            P(("groups", "tensor")),
        ),
        out_specs=P(("groups", "tensor"), None),
        check_vma=False,
    )
```

```python
import functools

import jax
import jax.numpy as jnp
from jax import lax
from jax.experimental import pallas as pl
from jax.experimental.pallas import tpu as pltpu
from jax.sharding import PartitionSpec as P

MIB = 1 << 20
VMEM = pl.BlockSpec(memory_space=pltpu.VMEM)
HBM = pl.BlockSpec(memory_space=pltpu.HBM)
ANY = pl.BlockSpec(memory_space=pl.ANY)
BLOCKS = 4
CHUNKS = 2


def cost(flops, moved):
    return pl.CostEstimate(flops=flops, bytes_accessed=moved, transcendentals=0)


def load_kernel(start, source, *rest):
    piece, token, sem = rest[-3:]
    copy = pltpu.make_async_copy(source.at[pl.ds(start, piece.shape[0])], piece, sem)
    copy.start()
    token[...] = jnp.zeros_like(token)
    copy.wait()


def load(source, after, start, rows):
    shape = (rows, source.shape[1])
    return pl.pallas_call(
        functools.partial(load_kernel, start),
        out_shape=(pltpu.VMEM(shape, source.dtype), pltpu.VMEM((8, 128), jnp.float32)),
        in_specs=[HBM] + [ANY] * len(after),
        out_specs=(VMEM, VMEM),
        scratch_shapes=[pltpu.SemaphoreType.DMA],
        compiler_params=pltpu.CompilerParams(vmem_limit_bytes=1 * MIB),
        cost_estimate=cost(0, 2 * rows * source.shape[1]),
    )(source, *after)


def join_kernel(count, *refs):
    joined = refs[-1]
    at = 0
    for part in refs[:count]:
        joined[at : at + part.shape[0], :] = part[...]
        at += part.shape[0]


def join(parts, tokens):
    rows, width = sum(part.shape[0] for part in parts), parts[0].shape[1]
    return pl.pallas_call(
        functools.partial(join_kernel, len(parts)),
        out_shape=pltpu.VMEM((rows, width), parts[0].dtype),
        in_specs=[VMEM] * len(parts) + [ANY] * len(tokens),
        out_specs=VMEM,
        compiler_params=pltpu.CompilerParams(vmem_limit_bytes=2 * MIB),
        cost_estimate=cost(0, 4 * rows * width),
    )(*parts, *tokens)


def hidden_kernel(rows, mine, theirs, g0, u0, g1, u1, gate, up, down, hidden, d0, d1, d2, tokens, g2, u2, g3, u3, sems):
    def copy(source, block, into, sem):
        return pltpu.make_async_copy(source.at[pl.ds(block * rows, rows)], into, sems.at[sem])

    streamed = [
        copy(gate, 2, g2, 0),
        copy(up, 2, u2, 1),
        copy(gate, 3, g3, 2),
        copy(up, 3, u3, 3),
        copy(down, 0, d0, 4),
        copy(down, 1, d1, 5),
        copy(down, 2, d2, 6),
    ]
    streamed[0].start()
    streamed[1].start()
    half = mine.shape[0]
    tokens[:half, :] = mine[...]
    tokens[half:, :] = theirs[...]
    contract = (((1,), (1,)), ((), ()))

    def product(weight):
        return lax.dot_general(weight[...], tokens[...], contract, preferred_element_type=jnp.float32)

    def finish(block, gate_value, up_value):
        value = gate_value / (1.0 + jnp.exp(-gate_value)) * up_value
        hidden[block * rows : (block + 1) * rows, :] = value.astype(hidden.dtype)

    gate_value = product(g0)
    streamed[2].start()
    finish(0, gate_value, product(u0))
    streamed[3].start()
    gate_value = product(g1)
    streamed[4].start()
    finish(1, gate_value, product(u1))
    streamed[5].start()
    streamed[0].wait()
    gate_value = product(g2)
    streamed[6].start()
    streamed[1].wait()
    finish(2, gate_value, product(u2))
    streamed[2].wait()
    gate_value = product(g3)
    streamed[3].wait()
    finish(3, gate_value, product(u3))
    for one in streamed[4:]:
        one.wait()


def hidden_of(mine, theirs, pieces, gate, up, down):
    rows, width = pieces[0].shape
    count = mine.shape[0] + theirs.shape[0]
    block = pltpu.VMEM((rows, width), gate.dtype)
    return pl.pallas_call(
        functools.partial(hidden_kernel, rows),
        out_shape=(pltpu.VMEM((gate.shape[0], count), gate.dtype),) + (pltpu.VMEM((rows, width), gate.dtype),) * 3,
        in_specs=[VMEM] * 6 + [HBM] * 3,
        out_specs=(VMEM,) * 4,
        input_output_aliases={2: 1, 3: 2, 4: 3},
        scratch_shapes=[pltpu.VMEM((count, width), mine.dtype)] + [block] * 4 + [pltpu.SemaphoreType.DMA((7,))],
        compiler_params=pltpu.CompilerParams(vmem_limit_bytes=8 * rows * width + 7 * MIB),
        cost_estimate=cost(4 * count * gate.size, 4 * gate.size),
    )(*(pltpu.with_memory_space_constraint(one, pltpu.VMEM) for one in (mine, theirs, *pieces)), gate, up, down)


def down_kernel(start, hidden, d0, d1, d2, down, keep, send, d3, sem):
    rows, columns = d0.shape[0], keep.shape[1]
    half = keep.shape[0]
    copy = pltpu.make_async_copy(down.at[pl.ds(3 * rows, rows), pl.ds(start, columns)], d3, sem)
    copy.start()
    total = None
    for block, piece in enumerate((d0, d1, d2, d3)):
        if block == 3:
            copy.wait()
        value = lax.dot_general(
            hidden[block * rows : (block + 1) * rows, :],
            d3[...] if block == 3 else piece[:, start : start + columns],
            (((0,), (0,)), ((), ())),
            preferred_element_type=jnp.float32,
        )
        total = value if total is None else total + value
    keep[...] = total[:half]
    send[...] = total[half:].astype(send.dtype)


def down_of(hidden, pieces, down, start, columns):
    half = hidden.shape[1] // 2
    rows = pieces[0].shape[0]
    return pl.pallas_call(
        functools.partial(down_kernel, start),
        out_shape=(pltpu.VMEM((half, columns), jnp.float32), pltpu.VMEM((half, columns), jnp.bfloat16)),
        in_specs=[VMEM] * 4 + [HBM],
        out_specs=(VMEM, VMEM),
        scratch_shapes=[pltpu.VMEM((rows, columns), down.dtype), pltpu.SemaphoreType.DMA],
        compiler_params=pltpu.CompilerParams(vmem_limit_bytes=8 * MIB),
        cost_estimate=cost(4 * half * hidden.shape[0] * columns, 2 * hidden.shape[0] * columns),
    )(hidden, *pieces, down)


def fold_kernel(keep, came, kept, *sends):
    total = keep[...] + came[...].astype(jnp.float32)
    rows = kept.shape[0]
    kept[...] = total[:rows]
    for at, send in enumerate(sends):
        send[...] = total[(at + 1) * rows : (at + 2) * rows].astype(send.dtype)


def fold(keep, came, ways):
    rows, columns = keep.shape[0] // ways, keep.shape[1]
    return pl.pallas_call(
        fold_kernel,
        out_shape=(pltpu.VMEM((rows, columns), jnp.float32),)
        + (pltpu.VMEM((rows, columns), jnp.bfloat16),) * (ways - 1),
        in_specs=[VMEM, VMEM],
        out_specs=(VMEM,) * ways,
        compiler_params=pltpu.CompilerParams(vmem_limit_bytes=2 * MIB),
        cost_estimate=cost(0, 8 * keep.size),
    )(keep, came)


def exchange(array, mask, count):
    return lax.ppermute(array, "tensor", [(i, i ^ mask) for i in range(count)])


def masked(terms, own, valid_counts):
    keep = jnp.arange(own, dtype=jnp.int32)[:, None] < valid_counts[0]
    return jnp.where(keep, terms, 0.0).astype(jnp.bfloat16)


def reduced(keep, send, masks, count):
    for at, mask in enumerate(masks):
        total = keep + exchange(send, mask, count).astype(jnp.float32)
        if at + 1 == len(masks):
            return total
        rows = total.shape[0] // 2
        keep, send = total[:rows], total[rows:].astype(jnp.bfloat16)


def plain(count, masks, tokens, gate_weight, up_weight, down_weight, valid_counts):
    own = tokens.shape[0]
    gathered = tokens
    for mask in reversed(masks):
        gathered = jnp.concatenate([gathered, exchange(gathered, mask, count)], axis=0)
    gate_value = jnp.dot(gathered, gate_weight, preferred_element_type=jnp.float32)
    up_value = jnp.dot(gathered, up_weight, preferred_element_type=jnp.float32)
    hidden = (jax.nn.silu(gate_value) * up_value).astype(jnp.bfloat16)
    terms = jnp.dot(hidden, down_weight, preferred_element_type=jnp.float32)
    half = terms.shape[0] // 2
    total = reduced(terms[:half], terms[half:].astype(jnp.bfloat16), masks, count)
    return masked(total, own, valid_counts)


def per_device(count, masks, tokens, gate_weight, up_weight, down_weight, valid_counts):
    own, width = tokens.shape
    gate, up, down = (
        pltpu.with_memory_space_constraint(one, pltpu.HBM) for one in (gate_weight.T, up_weight.T, down_weight)
    )
    rows = gate.shape[0] // BLOCKS
    *single, far, farther = masks
    direct = [far, farther, far | farther]
    g0, token = load(gate, (), 0, rows)
    u0, other = load(up, (token,), 0, rows)
    mine = join([tokens] + [exchange(tokens, mask, count) for mask in direct], [token, other])
    pieces = [g0, u0]
    for mask, source in zip(reversed(single[1:]), (gate,)):
        theirs = exchange(mine, mask, count)
        piece, token = load(source, (mine,), rows, rows)
        pieces.append(piece)
        mine = join([mine, theirs], [token])
    theirs = exchange(mine, single[0], count)
    pieces.append(load(up, (mine,), rows, rows)[0])
    hidden, *down_pieces = hidden_of(mine, theirs, pieces, gate, up, down)
    columns = width // CHUNKS
    parts = []
    for chunk in range(CHUNKS):
        keep, send = down_of(hidden, down_pieces, down, chunk * columns, columns)
        for mask in single:
            ways = 4 if mask == single[-1] else 2
            keep, *sends = fold(keep, exchange(send, mask, count), ways)
            send = sends[0]
        for mask, send in zip(direct, sends):
            keep = keep + exchange(send, mask, count).astype(jnp.float32)
        parts.append(keep)
    return masked(jnp.concatenate(parts, axis=1), own, valid_counts)


def solution(mesh):
    count = mesh.shape["tensor"]
    masks = [1 << bit for bit in range(count.bit_length() - 1)]

    def step(tokens, gate_weight, up_weight, down_weight, valid_counts):
        hidden_rows, width = down_weight.shape
        fits = 8 * hidden_rows * width <= 2 * 56 * MIB
        whole_tiles = hidden_rows % (16 * BLOCKS) == 0 and width % (128 * CHUNKS) == 0
        small = (tokens.shape[0] << len(masks)) <= 64 and len(masks) == 4
        use = per_device if fits and whole_tiles and small else plain
        return use(count, masks, tokens, gate_weight, up_weight, down_weight, valid_counts)

    return jax.shard_map(
        step,
        mesh=mesh,
        in_specs=(
            P(("groups", "tensor"), None),
            P(None, "tensor"),
            P(None, "tensor"),
            P("tensor", None),
            P(("groups", "tensor")),
        ),
        out_specs=P(("groups", "tensor"), None),
        check_vma=False,
    )
```

```python
import functools

import jax
import jax.numpy as jnp
from jax import lax
from jax.experimental import pallas as pl
from jax.experimental.pallas import tpu as pltpu
from jax.sharding import PartitionSpec as P

MIB = 1 << 20
VMEM = pl.BlockSpec(memory_space=pltpu.VMEM)
HBM = pl.BlockSpec(memory_space=pltpu.HBM)
ANY = pl.BlockSpec(memory_space=pl.ANY)
BLOCKS = 4
CHUNKS = 2
DEPTH = 2048


def cost(flops, moved):
    return pl.CostEstimate(flops=flops, bytes_accessed=moved, transcendentals=0)


def load_kernel(start, source, *rest):
    piece, token, sem = rest[-3:]
    copy = pltpu.make_async_copy(source.at[pl.ds(start, piece.shape[0])], piece, sem)
    copy.start()
    token[...] = jnp.zeros_like(token)
    copy.wait()


def load(source, after, start, rows):
    shape = (rows, source.shape[1])
    return pl.pallas_call(
        functools.partial(load_kernel, start),
        out_shape=(pltpu.VMEM(shape, source.dtype), pltpu.VMEM((8, 128), jnp.float32)),
        in_specs=[HBM] + [ANY] * len(after),
        out_specs=(VMEM, VMEM),
        scratch_shapes=[pltpu.SemaphoreType.DMA],
        compiler_params=pltpu.CompilerParams(vmem_limit_bytes=1 * MIB),
        cost_estimate=cost(0, 2 * rows * source.shape[1]),
    )(source, *after)


def join_kernel(count, *refs):
    joined = refs[-1]
    at = 0
    for part in refs[:count]:
        joined[at : at + part.shape[0], :] = part[...]
        at += part.shape[0]


def join(parts, tokens):
    rows, width = sum(part.shape[0] for part in parts), parts[0].shape[1]
    return pl.pallas_call(
        functools.partial(join_kernel, len(parts)),
        out_shape=pltpu.VMEM((rows, width), parts[0].dtype),
        in_specs=[VMEM] * len(parts) + [ANY] * len(tokens),
        out_specs=VMEM,
        compiler_params=pltpu.CompilerParams(vmem_limit_bytes=2 * MIB),
        cost_estimate=cost(0, 4 * rows * width),
    )(*parts, *tokens)


def hidden_kernel(rows, mine, theirs, g0, u0, g1, u1, gate, up, down, h0, h1, h2, h3, d0, d1, d2, d3, tokens, g2, u2, g3, u3, sems):
    order = [
        (gate, 2, g2),
        (up, 2, u2),
        (gate, 3, g3),
        (up, 3, u3),
        (down, 0, d0),
        (down, 1, d1),
        (down, 2, d2),
        (down, 3, d3),
    ]
    copies = [
        pltpu.make_async_copy(source.at[pl.ds(block * rows, rows)], into, sems.at[at])
        for at, (source, block, into) in enumerate(order)
    ]
    copies[0].start()
    copies[1].start()
    half, width = mine.shape
    tokens[:half, :] = mine[...]
    tokens[half:, :] = theirs[...]

    def product(weight):
        total = None
        for at in range(0, width, DEPTH):
            value = lax.dot_general(
                tokens[:, at : min(at + DEPTH, width)],
                weight[:, at : min(at + DEPTH, width)],
                (((1,), (1,)), ((), ())),
                preferred_element_type=jnp.float32,
            )
            total = value if total is None else total + value
        return total

    def finish(hidden, gate_value, up_value):
        value = gate_value / (1.0 + jnp.exp(-gate_value)) * up_value
        hidden[...] = value.astype(hidden.dtype)

    gate_value = product(g0)
    copies[2].start()
    finish(h0, gate_value, product(u0))
    copies[3].start()
    copies[4].start()
    gate_value = product(g1)
    copies[5].start()
    finish(h1, gate_value, product(u1))
    copies[6].start()
    copies[0].wait()
    gate_value = product(g2)
    copies[7].start()
    copies[1].wait()
    finish(h2, gate_value, product(u2))
    copies[2].wait()
    gate_value = product(g3)
    copies[3].wait()
    finish(h3, gate_value, product(u3))
    for copy in copies[4:]:
        copy.wait()


def hidden_of(mine, theirs, pieces, gate, up, down):
    rows, width = pieces[0].shape
    count = mine.shape[0] + theirs.shape[0]
    return pl.pallas_call(
        functools.partial(hidden_kernel, rows),
        out_shape=(pltpu.VMEM((count, rows), gate.dtype),) * 4 + (pltpu.VMEM((rows, width), gate.dtype),) * 4,
        in_specs=[VMEM] * 6 + [HBM] * 3,
        out_specs=(VMEM,) * 8,
        input_output_aliases={2: 4, 3: 5, 4: 6, 5: 7},
        scratch_shapes=[pltpu.VMEM((count, width), mine.dtype)]
        + [pltpu.VMEM((rows, width), gate.dtype)] * 4
        + [pltpu.SemaphoreType.DMA((8,))],
        compiler_params=pltpu.CompilerParams(vmem_limit_bytes=8 * rows * width + 4 * MIB),
        cost_estimate=cost(4 * count * gate.size, 4 * gate.size),
    )(*(pltpu.with_memory_space_constraint(one, pltpu.VMEM) for one in (mine, theirs, *pieces)), gate, up, down)


def down_kernel(start, *refs):
    hidden, pieces, (keep, send) = refs[:4], refs[4:8], refs[8:]
    half, columns = keep.shape
    total = None
    for part, piece in zip(hidden, pieces):
        value = jnp.dot(part[...], piece[:, start : start + columns], preferred_element_type=jnp.float32)
        total = value if total is None else total + value
    keep[...] = total[:half]
    send[...] = total[half:].astype(send.dtype)


def down_of(hidden, pieces, start, columns):
    half = hidden[0].shape[0] // 2
    rows = pieces[0].shape[0]
    return pl.pallas_call(
        functools.partial(down_kernel, start),
        out_shape=(pltpu.VMEM((half, columns), jnp.float32), pltpu.VMEM((half, columns), jnp.bfloat16)),
        in_specs=[VMEM] * 8,
        out_specs=(VMEM, VMEM),
        compiler_params=pltpu.CompilerParams(vmem_limit_bytes=4 * MIB),
        cost_estimate=cost(16 * half * rows * columns, 8 * rows * columns),
    )(*(pltpu.with_memory_space_constraint(one, pltpu.VMEM) for one in (*hidden, *pieces)))


def fold_kernel(keep, came, kept, send):
    rows = kept.shape[0]
    kept[...] = keep[:rows, :] + came[:rows, :].astype(jnp.float32)
    send[...] = (keep[rows:, :] + came[rows:, :].astype(jnp.float32)).astype(send.dtype)


def fold(keep, came):
    rows, columns = keep.shape[0] // 2, keep.shape[1]
    return pl.pallas_call(
        fold_kernel,
        out_shape=(pltpu.VMEM((rows, columns), jnp.float32), pltpu.VMEM((rows, columns), jnp.bfloat16)),
        in_specs=[VMEM, VMEM],
        out_specs=(VMEM, VMEM),
        compiler_params=pltpu.CompilerParams(vmem_limit_bytes=2 * MIB),
        cost_estimate=cost(0, 8 * keep.size),
    )(keep, came)


def last_kernel(counts, *refs):
    out = refs[-1]
    at = 0
    for keep, came in zip(refs[:-1:2], refs[1:-1:2]):
        rows, columns = keep.shape
        total = keep[...] + came[...].astype(jnp.float32)
        position = lax.broadcasted_iota(jnp.int32, (rows, columns), 0)
        total = jnp.where(position < counts[0], total, 0.0)
        out[:, at : at + columns] = total.astype(out.dtype)
        at += columns


def last(counts, parts):
    columns = sum(keep.shape[1] for keep, _ in parts)
    flat = [one for part in parts for one in part]
    return pl.pallas_call(
        last_kernel,
        out_shape=jax.ShapeDtypeStruct((flat[0].shape[0], columns), jnp.bfloat16),
        in_specs=[pl.BlockSpec(memory_space=pltpu.SMEM)] + [VMEM] * len(flat),
        out_specs=VMEM,
        compiler_params=pltpu.CompilerParams(vmem_limit_bytes=2 * MIB),
        cost_estimate=cost(0, 8 * columns),
    )(counts, *flat)


def exchange(array, mask, count):
    return lax.ppermute(array, "tensor", [(i, i ^ mask) for i in range(count)])


def masked(terms, own, valid_counts):
    keep = jnp.arange(own, dtype=jnp.int32)[:, None] < valid_counts[0]
    return jnp.where(keep, terms, 0.0).astype(jnp.bfloat16)


def reduced(keep, send, masks, count):
    for at, mask in enumerate(masks):
        total = keep + exchange(send, mask, count).astype(jnp.float32)
        if at + 1 == len(masks):
            return total
        rows = total.shape[0] // 2
        keep, send = total[:rows], total[rows:].astype(jnp.bfloat16)


def plain(count, masks, tokens, gate_weight, up_weight, down_weight, valid_counts):
    own = tokens.shape[0]
    gathered = tokens
    for mask in reversed(masks):
        gathered = jnp.concatenate([gathered, exchange(gathered, mask, count)], axis=0)
    gate_value = jnp.dot(gathered, gate_weight, preferred_element_type=jnp.float32)
    up_value = jnp.dot(gathered, up_weight, preferred_element_type=jnp.float32)
    hidden = (jax.nn.silu(gate_value) * up_value).astype(jnp.bfloat16)
    terms = jnp.dot(hidden, down_weight, preferred_element_type=jnp.float32)
    half = terms.shape[0] // 2
    total = reduced(terms[:half], terms[half:].astype(jnp.bfloat16), masks, count)
    return masked(total, own, valid_counts)


def per_device(count, masks, tokens, gate_weight, up_weight, down_weight, valid_counts):
    own, width = tokens.shape
    gate, up, down = (
        pltpu.with_memory_space_constraint(one, pltpu.HBM) for one in (gate_weight.T, up_weight.T, down_weight)
    )
    rows = gate.shape[0] // BLOCKS
    wanted = [(gate, 0), (up, 0), (gate, rows), (up, rows)]
    mine, after, pieces = tokens, (), []
    for mask, (source, start) in zip(reversed(masks), wanted):
        theirs = exchange(mine, mask, count)
        piece, token = load(source, after, start, rows)
        pieces.append(piece)
        if len(pieces) < len(masks):
            mine = join([mine, theirs], [token])
            after = (mine,)
    down_inputs = hidden_of(mine, theirs, pieces, gate, up, down)
    columns = width // CHUNKS
    parts = []
    for chunk in range(CHUNKS):
        keep, send = down_of(down_inputs[:4], down_inputs[4:], chunk * columns, columns)
        for mask in masks[:-1]:
            keep, send = fold(keep, exchange(send, mask, count))
        parts.append((keep, exchange(send, masks[-1], count)))
    return last(valid_counts, parts)


def solution(mesh):
    count = mesh.shape["tensor"]
    masks = [1 << bit for bit in range(count.bit_length() - 1)]

    def step(tokens, gate_weight, up_weight, down_weight, valid_counts):
        hidden_rows, width = down_weight.shape
        fits = 8 * hidden_rows * width <= 2 * 56 * MIB
        whole_tiles = hidden_rows % (16 * BLOCKS) == 0 and width % (128 * CHUNKS) == 0
        small = (tokens.shape[0] << len(masks)) <= 64 and len(masks) == 4
        use = per_device if fits and whole_tiles and small else plain
        return use(count, masks, tokens, gate_weight, up_weight, down_weight, valid_counts)

    return jax.shard_map(
        step,
        mesh=mesh,
        in_specs=(
            P(("groups", "tensor"), None),
            P(None, "tensor"),
            P(None, "tensor"),
            P("tensor", None),
            P(("groups", "tensor")),
        ),
        out_specs=P(("groups", "tensor"), None),
        check_vma=False,
    )
```

```python
import functools

import jax
import jax.numpy as jnp
from jax import lax
from jax.experimental import pallas as pl
from jax.experimental.pallas import tpu as pltpu
from jax.sharding import PartitionSpec as P

MIB = 1 << 20
VMEM = pl.BlockSpec(memory_space=pltpu.VMEM)
HBM = pl.BlockSpec(memory_space=pltpu.HBM)
ANY = pl.BlockSpec(memory_space=pl.ANY)
BLOCKS = 2
CHUNKS = 2


def cost(flops, moved):
    return pl.CostEstimate(flops=flops, bytes_accessed=moved, transcendentals=0)


def load_kernel(start, share, source, *rest):
    piece, token, sem = rest[-3:]
    at = pl.multiple_of(lax.axis_index("groups") * share + start, 16)
    copy = pltpu.make_async_copy(source.at[pl.ds(at, piece.shape[0])], piece, sem)
    copy.start()
    token[...] = jnp.zeros_like(token)
    copy.wait()


def load(source, after, start, rows, share):
    shape = (rows, source.shape[1])
    return pl.pallas_call(
        functools.partial(load_kernel, start, share),
        out_shape=(pltpu.VMEM(shape, source.dtype), pltpu.VMEM((8, 128), jnp.float32)),
        in_specs=[HBM] + [ANY] * len(after),
        out_specs=(VMEM, VMEM),
        scratch_shapes=[pltpu.SemaphoreType.DMA],
        compiler_params=pltpu.CompilerParams(vmem_limit_bytes=1 * MIB),
        cost_estimate=cost(0, 2 * rows * source.shape[1]),
    )(source, *after)


def join_kernel(count, *refs):
    joined = refs[-1]
    at = 0
    for part in refs[:count]:
        joined[at : at + part.shape[0], :] = part[...]
        at += part.shape[0]


def join(parts, tokens):
    rows, width = sum(part.shape[0] for part in parts), parts[0].shape[1]
    return pl.pallas_call(
        functools.partial(join_kernel, len(parts)),
        out_shape=pltpu.VMEM((rows, width), parts[0].dtype),
        in_specs=[VMEM] * len(parts) + [ANY] * len(tokens),
        out_specs=VMEM,
        compiler_params=pltpu.CompilerParams(vmem_limit_bytes=2 * MIB),
        cost_estimate=cost(0, 4 * rows * width),
    )(*parts, *tokens)


def hidden_kernel(mine, theirs, *refs):
    pieces, hidden, tokens = refs[: 2 * BLOCKS], refs[2 * BLOCKS : -1], refs[-1]
    half = mine.shape[0]
    tokens[:half, :] = mine[...]
    tokens[half:, :] = theirs[...]
    for gate, up, out in zip(pieces[::2], pieces[1::2], hidden):
        gate_value, up_value = (
            lax.dot_general(
                tokens[...], weight[...], (((1,), (1,)), ((), ())), preferred_element_type=jnp.float32
            )
            for weight in (gate, up)
        )
        value = gate_value / (1.0 + jnp.exp(-gate_value)) * up_value
        out[...] = value.astype(out.dtype)


def hidden_of(mine, theirs, pieces):
    rows, width = pieces[0].shape
    count = mine.shape[0] + theirs.shape[0]
    return pl.pallas_call(
        hidden_kernel,
        out_shape=(pltpu.VMEM((count, rows), mine.dtype),) * BLOCKS,
        in_specs=[VMEM] * (2 + 2 * BLOCKS),
        out_specs=(VMEM,) * BLOCKS,
        scratch_shapes=[pltpu.VMEM((count, width), mine.dtype)],
        compiler_params=pltpu.CompilerParams(vmem_limit_bytes=12 * MIB),
        cost_estimate=cost(4 * BLOCKS * count * rows * width, 4 * BLOCKS * rows * width),
    )(*(pltpu.with_memory_space_constraint(one, pltpu.VMEM) for one in (mine, theirs, *pieces)))


def down_kernel(start, *refs):
    hidden, pieces, (keep, send) = refs[:BLOCKS], refs[BLOCKS:-2], refs[-2:]
    half, columns = keep.shape
    total = None
    for part, piece in zip(hidden, pieces):
        value = jnp.dot(part[...], piece[:, start : start + columns], preferred_element_type=jnp.float32)
        total = value if total is None else total + value
    keep[...] = total[:half]
    send[...] = total[half:].astype(send.dtype)


def down_of(hidden, pieces, start, columns):
    half = hidden[0].shape[0] // 2
    rows = pieces[0].shape[0]
    return pl.pallas_call(
        functools.partial(down_kernel, start),
        out_shape=(pltpu.VMEM((half, columns), jnp.float32), pltpu.VMEM((half, columns), jnp.bfloat16)),
        in_specs=[VMEM] * (2 * BLOCKS),
        out_specs=(VMEM, VMEM),
        compiler_params=pltpu.CompilerParams(vmem_limit_bytes=4 * MIB),
        cost_estimate=cost(4 * BLOCKS * half * rows * columns, 2 * BLOCKS * rows * columns),
    )(*(pltpu.with_memory_space_constraint(one, pltpu.VMEM) for one in (*hidden, *pieces)))


def fold_kernel(keep, came, kept, send):
    rows = kept.shape[0]
    kept[...] = keep[:rows, :] + came[:rows, :].astype(jnp.float32)
    send[...] = (keep[rows:, :] + came[rows:, :].astype(jnp.float32)).astype(send.dtype)


def fold(keep, came):
    rows, columns = keep.shape[0] // 2, keep.shape[1]
    return pl.pallas_call(
        fold_kernel,
        out_shape=(pltpu.VMEM((rows, columns), jnp.float32), pltpu.VMEM((rows, columns), jnp.bfloat16)),
        in_specs=[VMEM, VMEM],
        out_specs=(VMEM, VMEM),
        compiler_params=pltpu.CompilerParams(vmem_limit_bytes=2 * MIB),
        cost_estimate=cost(0, 8 * keep.size),
    )(keep, came)


def last_kernel(counts, *refs):
    out = refs[-1]
    at = 0
    for keep, came in zip(refs[:-1:2], refs[1:-1:2]):
        rows, columns = keep.shape
        total = keep[...] + came[...].astype(jnp.float32)
        position = lax.broadcasted_iota(jnp.int32, (rows, columns), 0)
        total = jnp.where(position < counts[0], total, 0.0)
        out[:, at : at + columns] = total.astype(out.dtype)
        at += columns


def last(counts, parts):
    columns = sum(keep.shape[1] for keep, _ in parts)
    flat = [one for part in parts for one in part]
    return pl.pallas_call(
        last_kernel,
        out_shape=jax.ShapeDtypeStruct((flat[0].shape[0], columns), jnp.bfloat16),
        in_specs=[pl.BlockSpec(memory_space=pltpu.SMEM)] + [VMEM] * len(flat),
        out_specs=VMEM,
        compiler_params=pltpu.CompilerParams(vmem_limit_bytes=2 * MIB),
        cost_estimate=cost(0, 8 * columns),
    )(counts, *flat)


def exchange(array, mask, count):
    if mask == 0:
        return lax.ppermute(array, "groups", [(0, 1), (1, 0)])
    return lax.ppermute(array, "tensor", [(i, i ^ mask) for i in range(count)])


def masked(terms, own, valid_counts):
    keep = jnp.arange(own, dtype=jnp.int32)[:, None] < valid_counts[0]
    return jnp.where(keep, terms, 0.0).astype(jnp.bfloat16)


def reduced(keep, send, masks, count):
    for at, mask in enumerate(masks):
        total = keep + exchange(send, mask, count).astype(jnp.float32)
        if at + 1 == len(masks):
            return total
        rows = total.shape[0] // 2
        keep, send = total[:rows], total[rows:].astype(jnp.bfloat16)


def plain(count, masks, tokens, gate_weight, up_weight, down_weight, valid_counts):
    own = tokens.shape[0]
    gathered = tokens
    for mask in reversed(masks):
        gathered = jnp.concatenate([gathered, exchange(gathered, mask, count)], axis=0)
    gate_value = jnp.dot(gathered, gate_weight, preferred_element_type=jnp.float32)
    up_value = jnp.dot(gathered, up_weight, preferred_element_type=jnp.float32)
    hidden = (jax.nn.silu(gate_value) * up_value).astype(jnp.bfloat16)
    terms = jnp.dot(hidden, down_weight, preferred_element_type=jnp.float32)
    half = terms.shape[0] // 2
    total = reduced(terms[:half], terms[half:].astype(jnp.bfloat16), masks, count)
    return masked(total, own, valid_counts)


def per_device(count, masks, tokens, gate_weight, up_weight, down_weight, valid_counts):
    own, width = tokens.shape
    gate, up, down = (
        pltpu.with_memory_space_constraint(one, pltpu.HBM) for one in (gate_weight.T, up_weight.T, down_weight)
    )
    share = gate.shape[0] // 2
    rows = share // BLOCKS
    wanted = [[(gate, 0)], [(up, 0)], [(gate, rows)], [(up, rows), (down, 0)], [(down, rows)]]
    masks = [*masks, 0]
    mine, after, pieces = tokens, (), []
    for step, (mask, sources) in enumerate(zip(reversed(masks), wanted)):
        theirs = exchange(mine, mask, count)
        tokens_of = []
        for source, start in sources:
            piece, token = load(source, after, start, rows, share)
            pieces.append(piece)
            tokens_of.append(token)
        if step + 1 < len(masks):
            mine = join([mine, theirs], tokens_of)
            after = (mine,)
    hidden = hidden_of(mine, theirs, pieces[: 2 * BLOCKS])
    columns = width // CHUNKS
    parts = []
    for chunk in range(CHUNKS):
        keep, send = down_of(hidden, pieces[2 * BLOCKS :], chunk * columns, columns)
        for mask in masks[:-1]:
            keep, send = fold(keep, exchange(send, mask, count))
        parts.append((keep, exchange(send, masks[-1], count)))
    return last(valid_counts, parts)


def solution(mesh):
    count = mesh.shape["tensor"]
    masks = [1 << bit for bit in range(count.bit_length() - 1)]

    def step(tokens, gate_weight, up_weight, down_weight, valid_counts):
        hidden_rows, width = down_weight.shape
        fits = 3 * hidden_rows * width <= 44 * MIB
        whole_tiles = hidden_rows % (2 * 16 * BLOCKS) == 0 and width % (128 * CHUNKS) == 0
        small = (tokens.shape[0] << len(masks)) <= 64 and len(masks) == 4 and mesh.shape["groups"] == 2
        use = per_device if fits and whole_tiles and small else plain
        return use(count, masks, tokens, gate_weight, up_weight, down_weight, valid_counts)

    return jax.shard_map(
        step,
        mesh=mesh,
        in_specs=(
            P(("groups", "tensor"), None),
            P(None, "tensor"),
            P(None, "tensor"),
            P("tensor", None),
            P(("groups", "tensor")),
        ),
        out_specs=P(("groups", "tensor"), None),
        check_vma=False,
    )
```

```python
import functools

import jax
import jax.numpy as jnp
from jax import lax
from jax.experimental import pallas as pl
from jax.experimental.pallas import tpu as pltpu
from jax.sharding import PartitionSpec as P

MIB = 1 << 20
VMEM = pl.BlockSpec(memory_space=pltpu.VMEM)
HBM = pl.BlockSpec(memory_space=pltpu.HBM)
ANY = pl.BlockSpec(memory_space=pl.ANY)
BLOCKS = 2
CHUNKS = 2


def cost(flops, moved):
    return pl.CostEstimate(flops=flops, bytes_accessed=moved, transcendentals=0)


def load_kernel(start, share, source, *rest):
    piece, token, sem = rest[-3:]
    at = pl.multiple_of(lax.axis_index("groups") * share + start, 16)
    copy = pltpu.make_async_copy(source.at[pl.ds(at, piece.shape[0])], piece, sem)
    copy.start()
    token[...] = jnp.zeros_like(token)
    copy.wait()


def load(source, after, start, rows, share):
    shape = (rows, source.shape[1])
    return pl.pallas_call(
        functools.partial(load_kernel, start, share),
        out_shape=(pltpu.VMEM(shape, source.dtype), pltpu.VMEM((8, 128), jnp.float32)),
        in_specs=[HBM] + [ANY] * len(after),
        out_specs=(VMEM, VMEM),
        scratch_shapes=[pltpu.SemaphoreType.DMA],
        compiler_params=pltpu.CompilerParams(vmem_limit_bytes=1 * MIB),
        cost_estimate=cost(0, 2 * rows * source.shape[1]),
    )(source, *after)


def join_kernel(count, *refs):
    joined = refs[-1]
    at = 0
    for part in refs[:count]:
        joined[at : at + part.shape[0], :] = part[...]
        at += part.shape[0]


def join(parts, tokens):
    rows, width = sum(part.shape[0] for part in parts), parts[0].shape[1]
    return pl.pallas_call(
        functools.partial(join_kernel, len(parts)),
        out_shape=pltpu.VMEM((rows, width), parts[0].dtype),
        in_specs=[VMEM] * len(parts) + [ANY] * len(tokens),
        out_specs=VMEM,
        compiler_params=pltpu.CompilerParams(vmem_limit_bytes=2 * MIB),
        cost_estimate=cost(0, 4 * rows * width),
    )(*parts, *tokens)


def hidden_kernel(share, mine, theirs, *refs):
    pieces, down, refs = refs[: 2 * BLOCKS], refs[2 * BLOCKS], refs[2 * BLOCKS + 1 :]
    hidden, brought, (tokens, sems) = refs[:BLOCKS], refs[BLOCKS:-2], refs[-2:]
    rows = pieces[0].shape[0]
    first = lax.axis_index("groups") * share
    copies = [
        pltpu.make_async_copy(
            down.at[pl.ds(pl.multiple_of(first + block * rows, 16), rows)], into, sems.at[block]
        )
        for block, into in enumerate(brought)
    ]
    for copy in copies:
        copy.start()
    half = mine.shape[0]
    tokens[:half, :] = mine[...]
    tokens[half:, :] = theirs[...]
    for gate, up, out in zip(pieces[::2], pieces[1::2], hidden):
        gate_value, up_value = (
            lax.dot_general(
                tokens[...], weight[...], (((1,), (1,)), ((), ())), preferred_element_type=jnp.float32
            )
            for weight in (gate, up)
        )
        value = gate_value / (1.0 + jnp.exp(-gate_value)) * up_value
        out[...] = value.astype(out.dtype)
    for copy in copies:
        copy.wait()


def hidden_of(mine, theirs, pieces, down, share):
    rows, width = pieces[0].shape
    count = mine.shape[0] + theirs.shape[0]
    return pl.pallas_call(
        functools.partial(hidden_kernel, share),
        out_shape=(pltpu.VMEM((count, rows), mine.dtype),) * BLOCKS + (pltpu.VMEM((rows, width), down.dtype),) * BLOCKS,
        in_specs=[VMEM] * (2 + 2 * BLOCKS) + [HBM],
        out_specs=(VMEM,) * (2 * BLOCKS),
        scratch_shapes=[pltpu.VMEM((count, width), mine.dtype), pltpu.SemaphoreType.DMA((BLOCKS,))],
        compiler_params=pltpu.CompilerParams(vmem_limit_bytes=12 * MIB),
        cost_estimate=cost(4 * BLOCKS * count * rows * width, 6 * BLOCKS * rows * width),
    )(*(pltpu.with_memory_space_constraint(one, pltpu.VMEM) for one in (mine, theirs, *pieces)), down)


def down_kernel(start, *refs):
    hidden, pieces, (keep, send) = refs[:BLOCKS], refs[BLOCKS:-2], refs[-2:]
    half, columns = keep.shape
    total = None
    for part, piece in zip(hidden, pieces):
        value = jnp.dot(part[...], piece[:, start : start + columns], preferred_element_type=jnp.float32)
        total = value if total is None else total + value
    keep[...] = total[:half]
    send[...] = total[half:].astype(send.dtype)


def down_of(hidden, pieces, start, columns):
    half = hidden[0].shape[0] // 2
    rows = pieces[0].shape[0]
    return pl.pallas_call(
        functools.partial(down_kernel, start),
        out_shape=(pltpu.VMEM((half, columns), jnp.float32), pltpu.VMEM((half, columns), jnp.bfloat16)),
        in_specs=[VMEM] * (2 * BLOCKS),
        out_specs=(VMEM, VMEM),
        compiler_params=pltpu.CompilerParams(vmem_limit_bytes=4 * MIB),
        cost_estimate=cost(4 * BLOCKS * half * rows * columns, 2 * BLOCKS * rows * columns),
    )(*(pltpu.with_memory_space_constraint(one, pltpu.VMEM) for one in (*hidden, *pieces)))


def fold_kernel(swapped, keep, came, kept, send):
    total = keep[...] + came[...].astype(jnp.float32)
    rows = kept.shape[0]
    if swapped:
        part = rows // 2
        for at in range(2):
            start = 2 * at * part
            kept[at * part : (at + 1) * part, :] = total[start : start + part]
        send[...] = jnp.concatenate(
            [total[part : 2 * part], total[3 * part : 4 * part]], axis=0
        ).astype(send.dtype)
    else:
        kept[...] = total[:rows]
        send[...] = total[rows:].astype(send.dtype)


def fold(keep, came, swapped):
    rows, columns = keep.shape[0] // 2, keep.shape[1]
    return pl.pallas_call(
        functools.partial(fold_kernel, swapped),
        out_shape=(pltpu.VMEM((rows, columns), jnp.float32), pltpu.VMEM((rows, columns), jnp.bfloat16)),
        in_specs=[VMEM, VMEM],
        out_specs=(VMEM, VMEM),
        compiler_params=pltpu.CompilerParams(vmem_limit_bytes=4 * MIB),
        cost_estimate=cost(0, 8 * keep.size),
    )(keep, came)


def last_kernel(counts, *refs):
    out = refs[-1]
    at = 0
    for keep, came in zip(refs[:-1:2], refs[1:-1:2]):
        rows, columns = keep.shape
        total = keep[...] + came[...].astype(jnp.float32)
        position = lax.broadcasted_iota(jnp.int32, (rows, columns), 0)
        total = jnp.where(position < counts[0], total, 0.0)
        out[:, at : at + columns] = total.astype(out.dtype)
        at += columns


def last(counts, parts):
    columns = sum(keep.shape[1] for keep, _ in parts)
    flat = [one for part in parts for one in part]
    return pl.pallas_call(
        last_kernel,
        out_shape=jax.ShapeDtypeStruct((flat[0].shape[0], columns), jnp.bfloat16),
        in_specs=[pl.BlockSpec(memory_space=pltpu.SMEM)] + [VMEM] * len(flat),
        out_specs=VMEM,
        compiler_params=pltpu.CompilerParams(vmem_limit_bytes=2 * MIB),
        cost_estimate=cost(0, 8 * columns),
    )(counts, *flat)


def exchange(array, mask, count):
    if mask == 0:
        return lax.ppermute(array, "groups", [(0, 1), (1, 0)])
    return lax.ppermute(array, "tensor", [(i, i ^ mask) for i in range(count)])


def masked(terms, own, valid_counts):
    keep = jnp.arange(own, dtype=jnp.int32)[:, None] < valid_counts[0]
    return jnp.where(keep, terms, 0.0).astype(jnp.bfloat16)


def reduced(keep, send, masks, count):
    for at, mask in enumerate(masks):
        total = keep + exchange(send, mask, count).astype(jnp.float32)
        if at + 1 == len(masks):
            return total
        rows = total.shape[0] // 2
        keep, send = total[:rows], total[rows:].astype(jnp.bfloat16)


def plain(count, masks, tokens, gate_weight, up_weight, down_weight, valid_counts):
    own = tokens.shape[0]
    gathered = tokens
    for mask in reversed(masks):
        gathered = jnp.concatenate([gathered, exchange(gathered, mask, count)], axis=0)
    gate_value = jnp.dot(gathered, gate_weight, preferred_element_type=jnp.float32)
    up_value = jnp.dot(gathered, up_weight, preferred_element_type=jnp.float32)
    hidden = (jax.nn.silu(gate_value) * up_value).astype(jnp.bfloat16)
    terms = jnp.dot(hidden, down_weight, preferred_element_type=jnp.float32)
    half = terms.shape[0] // 2
    total = reduced(terms[:half], terms[half:].astype(jnp.bfloat16), masks, count)
    return masked(total, own, valid_counts)


def per_device(count, masks, tokens, gate_weight, up_weight, down_weight, valid_counts):
    own, width = tokens.shape
    gate, up, down = (
        pltpu.with_memory_space_constraint(one, pltpu.HBM) for one in (gate_weight.T, up_weight.T, down_weight)
    )
    share = gate.shape[0] // 2
    rows = share // BLOCKS
    wanted = [[(gate, 0)], [(up, 0)], [(gate, rows)], [(up, rows)], []]
    masks = [*masks, 0]
    mine, after, pieces = tokens, (), []
    for step, (mask, sources) in enumerate(zip(reversed(masks), wanted)):
        theirs = exchange(mine, mask, count)
        ends = []
        for source, start in sources:
            piece, end = load(source, after, start, rows, share)
            pieces.append(piece)
            ends.append(end)
        if step + 1 < len(masks):
            mine = join([mine, theirs], ends)
            after = (mine,)
    outs = hidden_of(mine, theirs, pieces, down, share)
    columns = width // CHUNKS
    parts = []
    for chunk in range(CHUNKS):
        keep, send = down_of(outs[:BLOCKS], outs[BLOCKS:], chunk * columns, columns)
        order = list(masks)
        swap = chunk % 2 == 1
        if swap:
            order[1], order[2] = order[2], order[1]
        for step, mask in enumerate(order[:-1]):
            keep, send = fold(keep, exchange(send, mask, count), swap and step == 0)
        parts.append((keep, exchange(send, order[-1], count)))
    return last(valid_counts, parts)


def solution(mesh):
    count = mesh.shape["tensor"]
    masks = [1 << bit for bit in range(count.bit_length() - 1)]

    def step(tokens, gate_weight, up_weight, down_weight, valid_counts):
        hidden_rows, width = down_weight.shape
        fits = 3 * hidden_rows * width <= 44 * MIB
        whole_tiles = hidden_rows % (2 * 16 * BLOCKS) == 0 and width % (128 * CHUNKS) == 0
        small = (tokens.shape[0] << len(masks)) <= 64 and len(masks) == 4 and mesh.shape["groups"] == 2
        use = per_device if fits and whole_tiles and small else plain
        return use(count, masks, tokens, gate_weight, up_weight, down_weight, valid_counts)

    return jax.shard_map(
        step,
        mesh=mesh,
        in_specs=(
            P(("groups", "tensor"), None),
            P(None, "tensor"),
            P(None, "tensor"),
            P("tensor", None),
            P(("groups", "tensor")),
        ),
        out_specs=P(("groups", "tensor"), None),
        check_vma=False,
    )
```

```python
import functools

import jax
import jax.numpy as jnp
from jax import lax
from jax.experimental import pallas as pl
from jax.experimental.pallas import tpu as pltpu
from jax.sharding import PartitionSpec as P

MIB = 1 << 20
VMEM = pl.BlockSpec(memory_space=pltpu.VMEM)
HBM = pl.BlockSpec(memory_space=pltpu.HBM)
ANY = pl.BlockSpec(memory_space=pl.ANY)
BLOCKS = 2
CHUNKS = 2


def cost(flops, moved):
    return pl.CostEstimate(flops=flops, bytes_accessed=moved, transcendentals=0)


def load_kernel(starts, share, *refs):
    count = len(starts)
    sources, pieces, token, sems = refs[:count], refs[-count - 2 : -2], refs[-2], refs[-1]
    first = lax.axis_index("groups") * share
    copies = [
        pltpu.make_async_copy(
            source.at[pl.ds(pl.multiple_of(first + start, 16), piece.shape[0])], piece, sems.at[at]
        )
        for at, (source, start, piece) in enumerate(zip(sources, starts, pieces))
    ]
    for copy in copies:
        copy.start()
    token[...] = jnp.zeros_like(token)
    for copy in copies:
        copy.wait()


def load(wanted, after, share):
    pieces = tuple(pltpu.VMEM((rows, source.shape[1]), source.dtype) for source, _, rows in wanted)
    moved = sum(2 * rows * source.shape[1] for source, _, rows in wanted)
    return pl.pallas_call(
        functools.partial(load_kernel, [start for _, start, _ in wanted], share),
        out_shape=(*pieces, pltpu.VMEM((8, 128), jnp.float32)),
        in_specs=[HBM] * len(wanted) + [ANY] * len(after),
        out_specs=(VMEM,) * (len(wanted) + 1),
        scratch_shapes=[pltpu.SemaphoreType.DMA((len(wanted),))],
        compiler_params=pltpu.CompilerParams(vmem_limit_bytes=1 * MIB),
        cost_estimate=cost(0, moved),
    )(*(source for source, _, _ in wanted), *after)


def join_kernel(count, *refs):
    joined = refs[-1]
    at = 0
    for part in refs[:count]:
        joined[at : at + part.shape[0], :] = part[...]
        at += part.shape[0]


def join(parts, tokens):
    rows, width = sum(part.shape[0] for part in parts), parts[0].shape[1]
    return pl.pallas_call(
        functools.partial(join_kernel, len(parts)),
        out_shape=pltpu.VMEM((rows, width), parts[0].dtype),
        in_specs=[VMEM] * len(parts) + [ANY] * len(tokens),
        out_specs=VMEM,
        compiler_params=pltpu.CompilerParams(vmem_limit_bytes=2 * MIB),
        cost_estimate=cost(0, 4 * rows * width),
    )(*parts, *tokens)


def hidden_kernel(mine, theirs, *refs):
    pieces, hidden, tokens = refs[: 2 * BLOCKS], refs[2 * BLOCKS : -1], refs[-1]
    half = mine.shape[0]
    tokens[:half, :] = mine[...]
    tokens[half:, :] = theirs[...]
    for gate, up, out in zip(pieces[::2], pieces[1::2], hidden):
        gate_value, up_value = (
            lax.dot_general(
                tokens[...], weight[...], (((1,), (1,)), ((), ())), preferred_element_type=jnp.float32
            )
            for weight in (gate, up)
        )
        value = gate_value / (1.0 + jnp.exp(-gate_value)) * up_value
        out[...] = value.astype(out.dtype)


def hidden_of(mine, theirs, pieces):
    width = mine.shape[1]
    rows = sum(piece.shape[0] for piece in pieces[::2])
    count = mine.shape[0] + theirs.shape[0]
    return pl.pallas_call(
        hidden_kernel,
        out_shape=tuple(pltpu.VMEM((count, piece.shape[0]), mine.dtype) for piece in pieces[::2]),
        in_specs=[VMEM] * (2 + 2 * BLOCKS),
        out_specs=(VMEM,) * BLOCKS,
        scratch_shapes=[pltpu.VMEM((count, width), mine.dtype)],
        compiler_params=pltpu.CompilerParams(vmem_limit_bytes=12 * MIB),
        cost_estimate=cost(4 * count * rows * width, 4 * rows * width),
    )(*(pltpu.with_memory_space_constraint(one, pltpu.VMEM) for one in (mine, theirs, *pieces)))


def down_kernel(start, *refs):
    hidden, pieces, (keep, send) = refs[:BLOCKS], refs[BLOCKS:-2], refs[-2:]
    half, columns = keep.shape
    total = None
    for part, piece in zip(hidden, pieces):
        value = jnp.dot(part[...], piece[:, start : start + columns], preferred_element_type=jnp.float32)
        total = value if total is None else total + value
    keep[...] = total[:half]
    send[...] = total[half:].astype(send.dtype)


def down_of(hidden, pieces, start, columns):
    half = hidden[0].shape[0] // 2
    rows = sum(piece.shape[0] for piece in pieces)
    return pl.pallas_call(
        functools.partial(down_kernel, start),
        out_shape=(pltpu.VMEM((half, columns), jnp.float32), pltpu.VMEM((half, columns), jnp.bfloat16)),
        in_specs=[VMEM] * (2 * BLOCKS),
        out_specs=(VMEM, VMEM),
        compiler_params=pltpu.CompilerParams(vmem_limit_bytes=4 * MIB),
        cost_estimate=cost(4 * half * rows * columns, 2 * rows * columns),
    )(*(pltpu.with_memory_space_constraint(one, pltpu.VMEM) for one in (*hidden, *pieces)))


def fold_kernel(keep, came, kept, send):
    total = keep[...] + came[...].astype(jnp.float32)
    rows = kept.shape[0]
    kept[...] = total[:rows]
    send[...] = total[rows:].astype(send.dtype)


def fold(keep, came):
    rows, columns = keep.shape[0] // 2, keep.shape[1]
    return pl.pallas_call(
        fold_kernel,
        out_shape=(pltpu.VMEM((rows, columns), jnp.float32), pltpu.VMEM((rows, columns), jnp.bfloat16)),
        in_specs=[VMEM, VMEM],
        out_specs=(VMEM, VMEM),
        compiler_params=pltpu.CompilerParams(vmem_limit_bytes=4 * MIB),
        cost_estimate=cost(0, 8 * keep.size),
    )(keep, came)


def last_kernel(counts, *refs):
    out = refs[-1]
    at = 0
    for keep, came in zip(refs[:-1:2], refs[1:-1:2]):
        rows, columns = keep.shape
        total = keep[...] + came[...].astype(jnp.float32)
        position = lax.broadcasted_iota(jnp.int32, (rows, columns), 0)
        total = jnp.where(position < counts[0], total, 0.0)
        out[:, at : at + columns] = total.astype(out.dtype)
        at += columns


def last(counts, parts):
    columns = sum(keep.shape[1] for keep, _ in parts)
    flat = [one for part in parts for one in part]
    return pl.pallas_call(
        last_kernel,
        out_shape=jax.ShapeDtypeStruct((flat[0].shape[0], columns), jnp.bfloat16),
        in_specs=[pl.BlockSpec(memory_space=pltpu.SMEM)] + [VMEM] * len(flat),
        out_specs=VMEM,
        compiler_params=pltpu.CompilerParams(vmem_limit_bytes=2 * MIB),
        cost_estimate=cost(0, 8 * columns),
    )(counts, *flat)


def exchange(array, masks, count):
    pairs = [(i, i ^ masks[i % 2]) for i in range(2 * count)]
    return lax.ppermute(array, ("groups", "tensor"), pairs)


def masked(terms, own, valid_counts):
    keep = jnp.arange(own, dtype=jnp.int32)[:, None] < valid_counts[0]
    return jnp.where(keep, terms, 0.0).astype(jnp.bfloat16)


def plain(count, masks, tokens, gate_weight, up_weight, down_weight, valid_counts):
    own = tokens.shape[0]
    gathered = lax.all_gather(tokens, "tensor", axis=0, tiled=True)
    gate_value = jnp.dot(gathered, gate_weight, preferred_element_type=jnp.float32)
    up_value = jnp.dot(gathered, up_weight, preferred_element_type=jnp.float32)
    hidden = (jax.nn.silu(gate_value) * up_value).astype(jnp.bfloat16)
    terms = jnp.dot(hidden, down_weight, preferred_element_type=jnp.float32)
    return masked(lax.psum_scatter(terms, "tensor", scatter_dimension=0, tiled=True), own, valid_counts)


def per_device(count, masks, tokens, gate_weight, up_weight, down_weight, valid_counts):
    own, width = tokens.shape
    gate, up, down = (
        pltpu.with_memory_space_constraint(one, pltpu.HBM) for one in (gate_weight.T, up_weight.T, down_weight)
    )
    share = gate.shape[0] // 2
    first = second = share // BLOCKS
    wanted = [
        [(gate, 0, first)],
        [(up, 0, first)],
        [(gate, first, second)],
        [(up, first, second), (down, 0, first)],
        [(down, first, second)],
    ]
    core, y, near, far = masks
    x = count
    masks = [(core, core), (y, x), (x, y), (near, near), (far, far)]
    mine, after, loaded = tokens, (), []
    for step, (mask, sources) in enumerate(zip(reversed(masks), wanted)):
        theirs = exchange(mine, mask, count)
        *pieces, end = load(sources, after, share)
        loaded += pieces
        if step + 1 < len(masks):
            mine = join([mine, theirs], [end])
            after = (mine,)
    g0, u0, g1, u1, d0, d1 = loaded
    hidden = hidden_of(mine, theirs, [g0, u0, g1, u1])
    columns = width // CHUNKS
    parts = []
    for chunk in range(CHUNKS):
        keep, send = down_of(hidden, (d0, d1), chunk * columns, columns)
        for mask in masks[:-1]:
            keep, send = fold(keep, exchange(send, mask, count))
        parts.append((keep, exchange(send, masks[-1], count)))
    return last(valid_counts, parts)


def solution(mesh):
    count = mesh.shape["tensor"]
    masks = [1 << bit for bit in range(count.bit_length() - 1)]

    def step(tokens, gate_weight, up_weight, down_weight, valid_counts):
        hidden_rows, width = down_weight.shape
        fits = 3 * hidden_rows * width <= 44 * MIB
        whole_tiles = hidden_rows % (2 * 16 * BLOCKS) == 0 and width % (128 * CHUNKS) == 0
        small = (tokens.shape[0] << len(masks)) <= 64 and len(masks) == 4 and mesh.shape["groups"] == 2
        use = per_device if fits and whole_tiles and small else plain
        return use(count, masks, tokens, gate_weight, up_weight, down_weight, valid_counts)

    return jax.shard_map(
        step,
        mesh=mesh,
        in_specs=(
            P(("groups", "tensor"), None),
            P(None, "tensor"),
            P(None, "tensor"),
            P("tensor", None),
            P(("groups", "tensor")),
        ),
        out_specs=P(("groups", "tensor"), None),
        check_vma=False,
    )
```

```python
import functools

import jax
import jax.numpy as jnp
from jax import lax
from jax.experimental import pallas as pl
from jax.experimental.pallas import tpu as pltpu
from jax.sharding import PartitionSpec as P

MIB = 1 << 20
VMEM = pl.BlockSpec(memory_space=pltpu.VMEM)
HBM = pl.BlockSpec(memory_space=pltpu.HBM)
ANY = pl.BlockSpec(memory_space=pl.ANY)
BLOCKS = 2
CHUNKS = 2
APART = 4


def cost(flops, moved):
    return pl.CostEstimate(flops=flops, bytes_accessed=moved, transcendentals=0)


def load_kernel(starts, share, *refs):
    count = len(starts)
    sources, pieces, token, sems = refs[:count], refs[-count - 2 : -2], refs[-2], refs[-1]
    first = lax.axis_index("groups") * share
    copies = [
        pltpu.make_async_copy(
            source.at[pl.ds(pl.multiple_of(first + start, 16), piece.shape[0])], piece, sems.at[at]
        )
        for at, (source, start, piece) in enumerate(zip(sources, starts, pieces))
    ]
    for copy in copies:
        copy.start()
    token[...] = jnp.zeros_like(token)
    for copy in copies:
        copy.wait()


def load(wanted, after, share):
    pieces = tuple(pltpu.VMEM((rows, source.shape[1]), source.dtype) for source, _, rows in wanted)
    moved = sum(2 * rows * source.shape[1] for source, _, rows in wanted)
    return pl.pallas_call(
        functools.partial(load_kernel, [start for _, start, _ in wanted], share),
        out_shape=(*pieces, pltpu.VMEM((8, 128), jnp.float32)),
        in_specs=[HBM] * len(wanted) + [ANY] * len(after),
        out_specs=(VMEM,) * (len(wanted) + 1),
        scratch_shapes=[pltpu.SemaphoreType.DMA((len(wanted),))],
        compiler_params=pltpu.CompilerParams(vmem_limit_bytes=1 * MIB),
        cost_estimate=cost(0, moved),
    )(*(source for source, _, _ in wanted), *after)


def join_kernel(count, *refs):
    joined = refs[-1]
    at = 0
    for part in refs[:count]:
        joined[at : at + part.shape[0], :] = part[...]
        at += part.shape[0]


def join(parts, tokens):
    rows, width = sum(part.shape[0] for part in parts), parts[0].shape[1]
    return pl.pallas_call(
        functools.partial(join_kernel, len(parts)),
        out_shape=pltpu.VMEM((rows, width), parts[0].dtype),
        in_specs=[VMEM] * len(parts) + [ANY] * len(tokens),
        out_specs=VMEM,
        compiler_params=pltpu.CompilerParams(vmem_limit_bytes=2 * MIB),
        cost_estimate=cost(0, 4 * rows * width),
    )(*parts, *tokens)


def hidden_kernel(mine, theirs, *refs):
    pieces, hidden, tokens = refs[: 2 * BLOCKS], refs[2 * BLOCKS : -1], refs[-1]
    half = mine.shape[0]
    tokens[:half, :] = mine[...]
    tokens[half:, :] = theirs[...]
    for gate, up, out in zip(pieces[::2], pieces[1::2], hidden):
        gate_value, up_value = (
            lax.dot_general(
                tokens[...], weight[...], (((1,), (1,)), ((), ())), preferred_element_type=jnp.float32
            )
            for weight in (gate, up)
        )
        value = gate_value / (1.0 + jnp.exp(-gate_value)) * up_value
        out[...] = value.astype(out.dtype)


def hidden_of(mine, theirs, pieces):
    width = mine.shape[1]
    rows = sum(piece.shape[0] for piece in pieces[::2])
    count = mine.shape[0] + theirs.shape[0]
    return pl.pallas_call(
        hidden_kernel,
        out_shape=tuple(pltpu.VMEM((count, piece.shape[0]), mine.dtype) for piece in pieces[::2]),
        in_specs=[VMEM] * (2 + 2 * BLOCKS),
        out_specs=(VMEM,) * BLOCKS,
        scratch_shapes=[pltpu.VMEM((count, width), mine.dtype)],
        compiler_params=pltpu.CompilerParams(vmem_limit_bytes=12 * MIB),
        cost_estimate=cost(4 * count * rows * width, 4 * rows * width),
    )(*(pltpu.with_memory_space_constraint(one, pltpu.VMEM) for one in (mine, theirs, *pieces)))


def down_kernel(start, *refs):
    hidden, pieces, (keep, send) = refs[:BLOCKS], refs[BLOCKS:-2], refs[-2:]
    half, columns = keep.shape
    total = None
    for part, piece in zip(hidden, pieces):
        value = jnp.dot(part[...], piece[:, start : start + columns], preferred_element_type=jnp.float32)
        total = value if total is None else total + value
    keep[...] = total[:half]
    send[...] = total[half:].astype(send.dtype)


def down_of(hidden, pieces, start, columns):
    half = hidden[0].shape[0] // 2
    rows = sum(piece.shape[0] for piece in pieces)
    return pl.pallas_call(
        functools.partial(down_kernel, start),
        out_shape=(pltpu.VMEM((half, columns), jnp.float32), pltpu.VMEM((half, columns), jnp.bfloat16)),
        in_specs=[VMEM] * (2 * BLOCKS),
        out_specs=(VMEM, VMEM),
        compiler_params=pltpu.CompilerParams(vmem_limit_bytes=4 * MIB),
        cost_estimate=cost(4 * half * rows * columns, 2 * rows * columns),
    )(*(pltpu.with_memory_space_constraint(one, pltpu.VMEM) for one in (*hidden, *pieces)))


def fold_kernel(*refs):
    parts, kept, send = refs[:-2], refs[-2], refs[-1]
    rows = kept.shape[0]
    at = 0
    for keep, came in zip(parts[::2], parts[1::2]):
        total = keep[...] + came[...].astype(jnp.float32)
        columns = total.shape[1]
        kept[:, at : at + columns] = total[:rows]
        send[:, at : at + columns] = total[rows:].astype(send.dtype)
        at += columns


def fold(*parts):
    flat = [one for part in parts for one in part]
    rows, columns = flat[0].shape[0] // 2, sum(one.shape[1] for one in flat[::2])
    return pl.pallas_call(
        fold_kernel,
        out_shape=(pltpu.VMEM((rows, columns), jnp.float32), pltpu.VMEM((rows, columns), jnp.bfloat16)),
        in_specs=[VMEM] * len(flat),
        out_specs=(VMEM, VMEM),
        compiler_params=pltpu.CompilerParams(vmem_limit_bytes=4 * MIB),
        cost_estimate=cost(0, 16 * rows * columns),
    )(*flat)


def last_kernel(counts, *refs):
    out = refs[-1]
    at = 0
    for keep, came in zip(refs[:-1:2], refs[1:-1:2]):
        rows, columns = keep.shape
        total = keep[...] + came[...].astype(jnp.float32)
        position = lax.broadcasted_iota(jnp.int32, (rows, columns), 0)
        total = jnp.where(position < counts[0], total, 0.0)
        out[:, at : at + columns] = total.astype(out.dtype)
        at += columns


def last(counts, parts):
    columns = sum(keep.shape[1] for keep, _ in parts)
    flat = [one for part in parts for one in part]
    return pl.pallas_call(
        last_kernel,
        out_shape=jax.ShapeDtypeStruct((flat[0].shape[0], columns), jnp.bfloat16),
        in_specs=[pl.BlockSpec(memory_space=pltpu.SMEM)] + [VMEM] * len(flat),
        out_specs=VMEM,
        compiler_params=pltpu.CompilerParams(vmem_limit_bytes=2 * MIB),
        cost_estimate=cost(0, 8 * columns),
    )(counts, *flat)


def exchange(array, masks, count):
    pairs = [(i, i ^ masks[i % 2]) for i in range(2 * count)]
    return lax.ppermute(array, ("groups", "tensor"), pairs)


def masked(terms, own, valid_counts):
    keep = jnp.arange(own, dtype=jnp.int32)[:, None] < valid_counts[0]
    return jnp.where(keep, terms, 0.0).astype(jnp.bfloat16)


def plain(count, masks, tokens, gate_weight, up_weight, down_weight, valid_counts):
    own = tokens.shape[0]
    gathered = lax.all_gather(tokens, "tensor", axis=0, tiled=True)
    gate_value = jnp.dot(gathered, gate_weight, preferred_element_type=jnp.float32)
    up_value = jnp.dot(gathered, up_weight, preferred_element_type=jnp.float32)
    hidden = (jax.nn.silu(gate_value) * up_value).astype(jnp.bfloat16)
    terms = jnp.dot(hidden, down_weight, preferred_element_type=jnp.float32)
    return masked(lax.psum_scatter(terms, "tensor", scatter_dimension=0, tiled=True), own, valid_counts)


def per_device(count, masks, tokens, gate_weight, up_weight, down_weight, valid_counts):
    own, width = tokens.shape
    gate, up, down = (
        pltpu.with_memory_space_constraint(one, pltpu.HBM) for one in (gate_weight.T, up_weight.T, down_weight)
    )
    share = gate.shape[0] // 2
    first = second = share // BLOCKS
    wanted = [
        [(gate, 0, first)],
        [(up, 0, first)],
        [(gate, first, second)],
        [(up, first, second), (down, 0, first)],
        [(down, first, second)],
    ]
    core, y, near, far = masks
    x = count
    masks = [(core, core), (y, x), (x, y), (near, near), (far, far)]
    mine, after, loaded = tokens, (), []
    for step, (mask, sources) in enumerate(zip(reversed(masks), wanted)):
        theirs = exchange(mine, mask, count)
        *pieces, end = load(sources, after, share)
        loaded += pieces
        if step + 1 < len(masks):
            mine = join([mine, theirs], [end])
            after = (mine,)
    g0, u0, g1, u1, d0, d1 = loaded
    hidden = hidden_of(mine, theirs, [g0, u0, g1, u1])
    columns = width // CHUNKS
    parts = []
    for chunk in range(CHUNKS):
        keep, send = down_of(hidden, (d0, d1), chunk * columns, columns)
        for mask in masks[: APART - 1]:
            keep, send = fold((keep, exchange(send, mask, count)))
        parts.append((keep, exchange(send, masks[APART - 1], count)))
    for mask in masks[APART:]:
        keep, send = fold(*parts)
        parts = [(keep, exchange(send, mask, count))]
    return last(valid_counts, parts)


def solution(mesh):
    count = mesh.shape["tensor"]
    masks = [1 << bit for bit in range(count.bit_length() - 1)]

    def step(tokens, gate_weight, up_weight, down_weight, valid_counts):
        hidden_rows, width = down_weight.shape
        fits = 3 * hidden_rows * width <= 44 * MIB
        whole_tiles = hidden_rows % (2 * 16 * BLOCKS) == 0 and width % (128 * CHUNKS) == 0
        small = (tokens.shape[0] << len(masks)) <= 64 and len(masks) == 4 and mesh.shape["groups"] == 2
        use = per_device if fits and whole_tiles and small else plain
        return use(count, masks, tokens, gate_weight, up_weight, down_weight, valid_counts)

    return jax.shard_map(
        step,
        mesh=mesh,
        in_specs=(
            P(("groups", "tensor"), None),
            P(None, "tensor"),
            P(None, "tensor"),
            P("tensor", None),
            P(("groups", "tensor")),
        ),
        out_specs=P(("groups", "tensor"), None),
        check_vma=False,
    )
```
